32 devices in a mesh: group: 2 (over x), owner: 16 (over z, y, core).
Axes of the slice: x: 2, y: 2, z: 4, core: 2. Of those that a mesh axis runs over, the one named last changes fastest.
Arguments:
- tokens: bfloat16 [4096, 2048], P(('group', 'owner')), parts along dimension 0, may hold values from -6 to 6
- cotangent: bfloat16 [4096, 2048], P(('group', 'owner')), parts along dimension 0, may hold values from -6 to 6
- route_ids: int32 [4096, 3], P('group'), parts along dimension 0, may hold values from 0 to 15, as said below
- gate_probs: float32 [4096, 3], P(('group', 'owner')), parts along dimension 0, may hold values from 0.05 to 1
- w_gate: bfloat16 [16, 2048, 384], P('owner'), may hold values from -0.125 to 0.125
- w_up: bfloat16 [16, 2048, 384], P('owner'), may hold values from -0.125 to 0.125
- w_down: bfloat16 [16, 384, 2048], P('owner'), may hold values from -0.3125 to 0.3125
Outputs:
- expert_out: bfloat16 [4096, 2048], P(('group', 'owner')), parts along dimension 0
- grad_tokens: bfloat16 [4096, 2048], P(('group', 'owner')), parts along dimension 0
- grad_gates: float32 [4096, 3], P(('group', 'owner')), parts along dimension 0
- grad_w_gate: bfloat16 [32, 2048, 384], P(('group', 'owner')), parts along dimension 0
- grad_w_up: bfloat16 [32, 2048, 384], P(('group', 'owner')), parts along dimension 0
- grad_w_down: bfloat16 [32, 384, 2048], P(('group', 'owner')), parts along dimension 0
The draws below stay inside these ranges and needn't reach their ends.
There are 2 independent parts, one for each index of `group`. The reference program is written for one: setup_inputs(seed, part) draws one part's arguments, and reference() takes and returns one part's arrays. A program takes and returns all parts, laid end to end along the dimension named above; an argument that names none is the same for every part. Nothing has to cross between parts.
Inputs may be any that keep to these rules, and one draw needn't show every extreme that they name: `route_ids`: each token names 3 different experts. The 128 tokens of one owner device (aligned blocks) name any one expert at most 48 times, and some expert exactly 48 times.
All inputs are finite; a program needn't handle non-finite values.
Results may differ from the reference program's by a relative error of at most 0.008.
Values may be sent and summed in bfloat16 or wider, within the bound.
A program may use at most 128 MiB of HBM per device.

```python
import math
import jax
import jax.numpy as jnp
from jax import lax

D = 2048
FFW = 384
TOK_DEV = 128
TOPW = 3
EXPERTS = 16
MOST = 48
TOKENS = 2048
N_OWNER = 16


def draw_route_ids(key, part):
    assign_block = TOK_DEV * TOPW
    block_count = TOKENS // TOK_DEV
    extra_count = (EXPERTS - 1) // 2
    cycle_length = EXPERTS - 1 + extra_count
    key_hot = jax.random.fold_in(key, 11)
    key_blocks = jax.random.fold_in(key, 23)
    hot_id = jax.random.randint(key_hot, (), 0, EXPERTS).astype(jnp.int32)

    def one_block(block_key):
        key_order = jax.random.fold_in(block_key, 1)
        key_tokens = jax.random.fold_in(block_key, 2)
        others = jax.random.permutation(key_order, EXPERTS - 1).astype(jnp.int32)
        others = others + (others >= hot_id).astype(jnp.int32)
        cycle = jnp.concatenate([others, others[:extra_count]])
        position = jnp.arange(assign_block, dtype=jnp.int32)
        rest = cycle[jnp.maximum(position - MOST, 0) % cycle_length]
        labels = jnp.where(position < MOST, hot_id, rest)
        runs = jnp.sort(labels)
        table = runs.reshape(TOPW, TOK_DEV).T
        token_order = jax.random.permutation(key_tokens, TOK_DEV)
        return table[token_order]
    block_keys = jax.random.split(key_blocks, block_count)
    blocks = jax.vmap(one_block)(block_keys)
    return blocks.reshape(TOKENS, TOPW).astype(jnp.int32)


def shard_levels(stream_key, extent, pieces, smallest, largest):
    loudness = 1.0
    for axis_at, blocks in pieces:
        heights = jax.random.uniform(jax.random.fold_in(jax.random.fold_in(stream_key, 6), axis_at), (blocks,), jnp.float32, smallest / len(pieces), largest / len(pieces))
        loudness = loudness * jnp.repeat(jnp.exp(heights), extent[axis_at] // blocks).reshape((-1,) + (1,) * (len(extent) - 1 - axis_at))
    return loudness


def noise(stream_key, dims, scale, reach, shards=(), kind=jnp.bfloat16):
    result = jax.random.normal(stream_key, dims, jnp.float32) * scale
    if len(shards) > 0:
        result = shard_levels(stream_key, dims, shards, -0.22, 0.18) * result
    return jnp.clip(result, min=-reach, max=reach).astype(kind)


def setup_inputs(seed: int = 0, part: int = 0) -> dict:
    splits = jax.random.split(jax.random.key(seed), 8)
    own_keys = jax.random.split(jax.random.fold_in(splits[7], part), 8)
    return {
        "tokens": noise(own_keys[0], (TOKENS, D), 1.0, 6.0, ((0, 16),)),
        "cotangent": noise(own_keys[1], (TOKENS, D), 1.0, 6.0, ((0, 16),)),
        "route_ids": draw_route_ids(jax.random.fold_in(jax.random.fold_in(splits[7], part), 71), part),
        "gate_probs": jnp.clip(jnp.exp(math.log(1.0) - 2.9957323 * jax.random.uniform(own_keys[3], (TOKENS, TOPW), jnp.float32) ** shard_levels(own_keys[3], (TOKENS, TOPW), ((0, 16),), -0.2, 0.2)), 0.05, 1.0),
        "w_gate": noise(splits[4], (EXPERTS, D, FFW), D ** -0.5, 0.125, ((0, 16),)),
        "w_up": noise(splits[5], (EXPERTS, D, FFW), D ** -0.5, 0.125, ((0, 16),)),
        "w_down": noise(splits[6], (EXPERTS, FFW, D), FFW ** -0.5, 0.3125, ((0, 16),)),
    }


def expert_pass(tokens_in, cotan_in, gate_w, up_w, down_w):
    gate_pre = jnp.dot(tokens_in, gate_w, preferred_element_type=jnp.float32)
    up_pre = jnp.dot(tokens_in, up_w, preferred_element_type=jnp.float32)
    gate_sig = jax.nn.sigmoid(gate_pre)
    gate_act = gate_pre * gate_sig
    hidden = (gate_act * up_pre).astype(jnp.bfloat16)
    expert_y = jnp.dot(hidden, down_w, preferred_element_type=jnp.float32).astype(jnp.bfloat16)
    d_hidden = jnp.dot(cotan_in, down_w.T, preferred_element_type=jnp.float32)
    grad_gate_pre = (d_hidden * up_pre * gate_sig * (1.0 + gate_pre * (1.0 - gate_sig))).astype(jnp.bfloat16)
    grad_up_pre = (d_hidden * gate_act).astype(jnp.bfloat16)
    expert_dx = (jnp.dot(grad_gate_pre, gate_w.T, preferred_element_type=jnp.float32)
                 + jnp.dot(grad_up_pre, up_w.T, preferred_element_type=jnp.float32)).astype(jnp.bfloat16)
    return expert_y, expert_dx, hidden, grad_gate_pre, grad_up_pre


def reference(tokens, cotangent, route_ids, gate_probs, w_gate, w_up, w_down):
    assign_count = TOKENS * TOPW
    capacity = MOST * N_OWNER
    flat_ids = route_ids.reshape(assign_count)
    zero_row = jnp.zeros((1, D), jnp.bfloat16)
    token_copies = jnp.concatenate([jnp.repeat(tokens, TOPW, axis=0), zero_row], axis=0)
    scaled_cot = (gate_probs[:, :, None] * cotangent[:, None, :].astype(jnp.float32)).astype(jnp.bfloat16)
    cotan_ext = jnp.concatenate([scaled_cot.reshape(assign_count, D), zero_row], axis=0)

    def per_expert(carried, expert):
        out_rows, back_rows = carried
        picked = jnp.nonzero(flat_ids == expert, size=capacity, fill_value=assign_count)[0].astype(jnp.int32)
        rows_in = token_copies[picked]
        cotan_in = cotan_ext[picked]
        expert_y, expert_dx, hidden, grad_gate_pre, grad_up_pre = expert_pass(
            rows_in, cotan_in, w_gate[expert], w_up[expert], w_down[expert])
        grad_gate = jnp.dot(rows_in.T, grad_gate_pre, preferred_element_type=jnp.float32).astype(jnp.bfloat16)
        grad_up = jnp.dot(rows_in.T, grad_up_pre, preferred_element_type=jnp.float32).astype(jnp.bfloat16)
        grad_down = jnp.dot(hidden.T, cotan_in, preferred_element_type=jnp.float32).astype(jnp.bfloat16)
        out_rows = out_rows.at[picked].set(expert_y, mode="drop")
        back_rows = back_rows.at[picked].set(expert_dx, mode="drop")
        return (out_rows, back_rows), (grad_gate, grad_up, grad_down)

    initial = (jnp.zeros((assign_count, D), jnp.bfloat16), jnp.zeros((assign_count, D), jnp.bfloat16))
    (out_rows, back_rows), (grad_w_gate, grad_w_up, grad_w_down) = lax.scan(
        per_expert, initial, jnp.arange(EXPERTS, dtype=jnp.int32))
    routed_y = out_rows.reshape(TOKENS, TOPW, D).astype(jnp.float32)
    expert_out = jnp.sum(gate_probs[:, :, None] * routed_y, axis=1).astype(jnp.bfloat16)
    grad_tokens = jnp.sum(back_rows.reshape(TOKENS, TOPW, D).astype(jnp.float32), axis=1).astype(jnp.bfloat16)
    grad_gates = jnp.sum(routed_y * cotangent[:, None, :].astype(jnp.float32), axis=2)
    return expert_out, grad_tokens, grad_gates, grad_w_gate, grad_w_up, grad_w_down
```

```python
import functools

import jax
import jax.numpy as jnp
from jax import lax
from jax.experimental import pallas as pl
from jax.experimental.pallas import tpu as pltpu
from jax.sharding import PartitionSpec as P


def expert_pass(tokens_in, cotan_in, gate_w, up_w, down_w):
    gate_pre = jnp.dot(tokens_in, gate_w, preferred_element_type=jnp.float32)
    up_pre = jnp.dot(tokens_in, up_w, preferred_element_type=jnp.float32)
    gate_sig = jax.nn.sigmoid(gate_pre)
    gate_act = gate_pre * gate_sig
    hidden = (gate_act * up_pre).astype(jnp.bfloat16)
    expert_y = jnp.dot(hidden, down_w, preferred_element_type=jnp.float32).astype(jnp.bfloat16)
    d_hidden = jnp.dot(cotan_in, down_w.T, preferred_element_type=jnp.float32)
    grad_gate_pre = (d_hidden * up_pre * gate_sig * (1.0 + gate_pre * (1.0 - gate_sig))).astype(
        jnp.bfloat16
    )
    grad_up_pre = (d_hidden * gate_act).astype(jnp.bfloat16)
    expert_dx = (
        jnp.dot(grad_gate_pre, gate_w.T, preferred_element_type=jnp.float32)
        + jnp.dot(grad_up_pre, up_w.T, preferred_element_type=jnp.float32)
    ).astype(jnp.bfloat16)
    return (expert_y, expert_dx, hidden, grad_gate_pre, grad_up_pre)


def local(tokens, cotangent, route_ids, gate_probs, w_gate, w_up, w_down):
    owner_count = lax.axis_size("owner")
    my_index = lax.axis_index("owner")
    token_rows, model_width = tokens.shape
    route_count = route_ids.shape[1]
    slot_depth = 2 * token_rows * route_count // owner_count
    assign_count = token_rows * route_count
    slot_total = owner_count * slot_depth
    expert_ids = jnp.arange(owner_count, dtype=jnp.int32)
    id_table = route_ids.reshape(owner_count, assign_count)
    my_routes = lax.dynamic_index_in_dim(id_table, my_index, 0, keepdims=False)
    one_hot = (my_routes[:, None] == expert_ids[None, :]).astype(jnp.int32)
    rank_within = jnp.sum((jnp.cumsum(one_hot, axis=0) - one_hot) * one_hot, axis=1)
    source_loads = jnp.sum((id_table == my_index).astype(jnp.int32), axis=1)
    scaled_cot = (gate_probs[:, :, None] * cotangent[:, None, :].astype(jnp.float32)).astype(
        jnp.bfloat16
    )
    token_copies = jnp.broadcast_to(tokens[:, None, :], (token_rows, route_count, model_width))
    zero_row = jnp.zeros((1, model_width), jnp.bfloat16)
    token_ext = jnp.concatenate([token_copies.reshape(assign_count, model_width), zero_row], axis=0)
    cotan_ext = jnp.concatenate([scaled_cot.reshape(assign_count, model_width), zero_row], axis=0)
    is_hot = jnp.zeros((assign_count,), dtype=bool)
    slot_target = jnp.where(is_hot, slot_total, my_routes * slot_depth + rank_within)
    slot_source = jnp.full((slot_total + 1,), assign_count, jnp.int32)
    slot_source = slot_source.at[slot_target].set(jnp.arange(assign_count, dtype=jnp.int32))[
        :slot_total
    ]
    send_tokens = token_ext[slot_source].reshape(owner_count, slot_depth, model_width)
    send_cotan = cotan_ext[slot_source].reshape(owner_count, slot_depth, model_width)
    got_tokens, got_cotan = (
        lax.all_to_all(send_tokens, "owner", split_axis=0, concat_axis=0, tiled=True),
        lax.all_to_all(send_cotan, "owner", split_axis=0, concat_axis=0, tiled=True),
    )
    live_slot = (jnp.arange(slot_depth, dtype=jnp.int32)[None, :] < source_loads[:, None]).reshape(
        slot_total
    )
    compact_pos = jnp.cumsum(live_slot.astype(jnp.int32)) - 1
    live_total = jnp.sum(source_loads)
    compact_from = jnp.full((slot_total,), slot_total, jnp.int32)
    compact_from = compact_from.at[jnp.where(live_slot, compact_pos, slot_total)].set(
        jnp.arange(slot_total, dtype=jnp.int32), mode="drop"
    )
    flat_tokens = jnp.concatenate([got_tokens.reshape(slot_total, model_width), zero_row], axis=0)
    flat_cotan = jnp.concatenate([got_cotan.reshape(slot_total, model_width), zero_row], axis=0)
    compact_tokens = flat_tokens[compact_from]
    compact_cotan = flat_cotan[compact_from]
    gate_w = w_gate[0]
    up_w = w_up[0]
    down_w = w_down[0]
    hidden_width = gate_w.shape[1]

    def block_step(turn_index, carried):
        out_rows, back_rows, grad_gate, grad_up, grad_down = carried
        row_start = turn_index * assign_count
        block_tokens = lax.dynamic_slice_in_dim(compact_tokens, row_start, assign_count, 0)
        block_cotan = lax.dynamic_slice_in_dim(compact_cotan, row_start, assign_count, 0)
        expert_y, expert_dx, hidden, grad_gate_pre, grad_up_pre = expert_pass(
            block_tokens, block_cotan, gate_w, up_w, down_w
        )
        out_rows = lax.dynamic_update_slice_in_dim(out_rows, expert_y, row_start, 0)
        back_rows = lax.dynamic_update_slice_in_dim(back_rows, expert_dx, row_start, 0)
        grad_gate = grad_gate + jnp.dot(
            block_tokens.T, grad_gate_pre, preferred_element_type=jnp.float32
        )
        grad_up = grad_up + jnp.dot(block_tokens.T, grad_up_pre, preferred_element_type=jnp.float32)
        grad_down = grad_down + jnp.dot(hidden.T, block_cotan, preferred_element_type=jnp.float32)
        return (out_rows, back_rows, grad_gate, grad_up, grad_down)

    turn_count = (live_total + assign_count - 1) // assign_count
    initial = (
        jnp.zeros((slot_total, model_width), jnp.bfloat16),
        jnp.zeros((slot_total, model_width), jnp.bfloat16),
        jnp.zeros((model_width, hidden_width), jnp.float32),
        jnp.zeros((model_width, hidden_width), jnp.float32),
        jnp.zeros((hidden_width, model_width), jnp.float32),
    )
    out_rows, back_rows, grad_gate, grad_up, grad_down = lax.fori_loop(
        0, turn_count, block_step, initial
    )
    return_pos = jnp.where(live_slot, compact_pos, 0)
    return_y = out_rows[return_pos].reshape(owner_count, slot_depth, model_width)
    return_dx = back_rows[return_pos].reshape(owner_count, slot_depth, model_width)
    came_y, came_dx = (
        lax.all_to_all(return_y, "owner", split_axis=0, concat_axis=0, tiled=True),
        lax.all_to_all(return_dx, "owner", split_axis=0, concat_axis=0, tiled=True),
    )
    pick_slot = jnp.where(is_hot, 0, slot_target)
    routed_rows = came_y.reshape(slot_total, model_width)[pick_slot]
    routed_backs = came_dx.reshape(slot_total, model_width)[pick_slot]
    grad_gate_out = grad_gate.astype(jnp.bfloat16)
    grad_up_out = grad_up.astype(jnp.bfloat16)
    grad_down_out = grad_down.astype(jnp.bfloat16)
    routed_y = routed_rows.reshape(token_rows, route_count, model_width).astype(jnp.float32)
    expert_out = jnp.sum(gate_probs[:, :, None] * routed_y, axis=1).astype(jnp.bfloat16)
    grad_tokens = jnp.sum(
        routed_backs.reshape(token_rows, route_count, model_width).astype(jnp.float32), axis=1
    ).astype(jnp.bfloat16)
    grad_gates = jnp.sum(routed_y * cotangent[:, None, :].astype(jnp.float32), axis=2)
    return (
        expert_out,
        grad_tokens,
        grad_gates,
        grad_gate_out[None],
        grad_up_out[None],
        grad_down_out[None],
    )


def ring_width(mesh):
    coords = [getattr(d, "coords", None) for d in mesh.devices.reshape(mesh.devices.shape[0], -1)[0]]
    if any(c is None for c in coords):
        return 2
    return 2 if len({c[1] for c in coords}) == 2 else 1


def ring_kernel(
    y_size, owners, cap,
    route_ref, prob_ref, tok_ref, cot_ref, wg_hbm, wu_hbm, wd_hbm,
    eo_ref, gt_ref, gg_ref, og_ref, ou_ref, od_ref,
    slots, probs, sib, sib_t, ring, ring_t, gates, sel_buf, rows, cot_rows, prow, back,
    hid, gpre, upre, wg_ref, wu_ref, wd_ref,
    ag_send, ag_recv, agt_send, agt_recv, sf_send, sf_recv, sft_send, sft_recv,
    sp_send, sp_recv, spt_send, spt_recv, rs_send, rs_recv, rst_send, rst_recv, loc,
):
    f32, bf16 = jnp.float32, jnp.bfloat16
    chips = owners // 2
    half = chips // 2
    depth = chips // y_size
    tok, width = tok_ref.shape
    me = lax.axis_index("owner")
    chip = me // 2
    core = me % 2
    if y_size == 2:
        cz, cy = chip // 2, chip % 2
        pos = (1 - cy) * cz + cy * (2 * depth - 1 - cz)
    else:
        pos = chip

    def owner_at(offset, core_index):
        p = (pos + offset + chips) % chips
        if y_size == 2:
            py = p // depth
            pz = (1 - py) * p + py * (2 * depth - 1 - p)
            return (pz * 2 + py) * 2 + core_index
        return p * 2 + core_index

    right, left, twin = owner_at(1, core), owner_at(-1, core), owner_at(0, 1 - core)

    loads = [
        pltpu.make_async_copy(tok_ref, slots.at[0, :, pl.ds(0, width)], loc.at[0]),
        pltpu.make_async_copy(cot_ref, slots.at[0, :, pl.ds(width, width)], loc.at[1]),
        pltpu.make_async_copy(prob_ref, probs.at[0], loc.at[2]),
        pltpu.make_async_copy(wg_hbm, wg_ref, loc.at[3]),
        pltpu.make_async_copy(wu_hbm, wu_ref, loc.at[4]),
        pltpu.make_async_copy(wd_hbm, wd_ref, loc.at[5]),
    ]
    for c in loads:
        c.start()
    barrier = pltpu.get_barrier_semaphore()
    for other in (right, left, twin):
        pl.semaphore_signal(
            barrier, inc=1, device_id={"owner": other}, device_id_type=pl.DeviceIdType.MESH
        )
    pl.semaphore_wait(barrier, 3)
    for c in loads[:3]:
        c.wait()

    def remote(src, dst, send, recv, to):
        return pltpu.make_async_remote_copy(
            src_ref=src, dst_ref=dst, send_sem=send, recv_sem=recv,
            device_id={"owner": to}, device_id_type=pl.DeviceIdType.MESH,
        )

    lo, hi = pl.ds(0, width), pl.ds(width, width)

    def gather_copies(s):
        a, b = (-(s - 1)) % chips, s - 1
        c, d = (-s) % chips, s
        i = s - 1
        if s < half:
            return [
                remote(slots.at[a], slots.at[c], ag_send.at[0, i], ag_recv.at[0, i], right),
                remote(slots.at[b], slots.at[d], ag_send.at[1, i], ag_recv.at[1, i], left),
                remote(probs.at[a], probs.at[c], agt_send.at[0, i], agt_recv.at[0, i], right),
                remote(probs.at[b], probs.at[d], agt_send.at[1, i], agt_recv.at[1, i], left),
            ]
        return [
            remote(slots.at[a, :, lo], slots.at[half, :, lo], ag_send.at[0, i], ag_recv.at[0, i], right),
            remote(slots.at[b, :, hi], slots.at[half, :, hi], ag_send.at[1, i], ag_recv.at[1, i], left),
            remote(probs.at[a], probs.at[half], agt_send.at[0, i], agt_recv.at[0, i], right),
        ]

    def twin_copies(o):
        return [
            remote(slots.at[o], slots.at[chips + o], sf_send.at[o], sf_recv.at[o], twin),
            remote(probs.at[o], probs.at[chips + o], sft_send.at[o], sft_recv.at[o], twin),
        ]

    def partial_copies(o):
        return [
            remote(slots.at[chips + o], sib.at[o], sp_send.at[o], sp_recv.at[o], twin),
            remote(gates.at[chips + o], sib_t.at[o], spt_send.at[o], spt_recv.at[o], twin),
        ]

    def offsets(d):
        return [d] if d in (0, half) else [(-d) % chips, d]

    first_row = [0] * (half + 1)
    for d in range(half):
        first_row[d + 1] = first_row[d] + 2 * cap * len(offsets(d))
    chunk = 512 if width % 512 == 0 else 128
    contract0 = (((0,), (0,)), ((), ()))
    contract1 = (((1,), (1,)), ((), ()))

    def cols(i, base=0):
        return pl.ds(pl.multiple_of(base + i * chunk, 128), chunk)

    def over_chunks(body, init=0):
        return lax.fori_loop(0, width // chunk, body, init)

    upper = (
        lax.broadcasted_iota(jnp.int32, (tok, tok), 0)
        <= lax.broadcasted_iota(jnp.int32, (tok, tok), 1)
    ).astype(bf16)

    def batch_slots(d):
        return [(o, core) for o in offsets(d)] + [(chips + o, 1 - core) for o in offsets(d)]

    def compute(d):
        r0 = first_row[d]
        entries = batch_slots(d)
        m = cap * len(entries)
        marks = []
        for i, (j, source_core) in enumerate(entries):
            owner = owner_at(j % chips, source_core)
            mark = (route_ref[owner] == me).astype(f32)
            hit = jnp.sum(mark, axis=0, keepdims=True)
            count = jnp.dot(
                jnp.broadcast_to(hit, (8, tok)).astype(bf16), upper, preferred_element_type=f32
            )[0:1]
            rank = jnp.where(hit > 0, count - 1, -1.0)
            sel = lax.broadcasted_iota(jnp.int32, (cap, tok), 0).astype(f32) == rank
            weight = jnp.sum(probs[j] * mark, axis=0, keepdims=True)
            prow[i * cap : (i + 1) * cap, :] = jnp.sum(
                jnp.where(sel, weight, 0.0), axis=1, keepdims=True
            )
            sel_buf[j] = sel.astype(bf16)
            marks.append((mark, sel))

            def pick(k, carry, i=i, j=j):
                s = sel_buf[j]
                rows[r0 + i * cap : r0 + (i + 1) * cap, cols(k)] = jnp.dot(
                    s, slots[j, :, cols(k)], preferred_element_type=f32
                ).astype(bf16)
                c = jnp.dot(s, slots[j, :, cols(k, width)], preferred_element_type=f32)
                cot_rows[i * cap : (i + 1) * cap, cols(k)] = c.astype(bf16)
                rows[r0 + i * cap : r0 + (i + 1) * cap, cols(k, width)] = (
                    c * prow[i * cap : (i + 1) * cap, :]
                ).astype(bf16)
                return carry

            over_chunks(pick)
        x = rows[r0 : r0 + m, 0:width]
        gate_pre = jnp.dot(x, wg_ref[...], preferred_element_type=f32)
        up_pre = jnp.dot(x, wu_ref[...], preferred_element_type=f32)
        sig = jax.nn.sigmoid(gate_pre)
        act = gate_pre * sig
        hid[r0 : r0 + m, :] = (act * up_pre).astype(bf16)
        d_hidden = lax.dot_general(
            rows[r0 : r0 + m, width : 2 * width], wd_ref[...], contract1,
            preferred_element_type=f32,
        )
        gpre[r0 : r0 + m, :] = (
            d_hidden * up_pre * sig * (1.0 + gate_pre * (1.0 - sig))
        ).astype(bf16)
        upre[r0 : r0 + m, :] = (d_hidden * act).astype(bf16)

        def produce(k, total):
            y = jnp.dot(
                hid[r0 : r0 + m, :], wd_ref[:, cols(k)], preferred_element_type=f32
            ).astype(bf16).astype(f32)
            back[0:m, cols(k)] = (y * prow[0:m, :]).astype(bf16)
            dx = lax.dot_general(
                gpre[r0 : r0 + m, :], wg_ref[cols(k), :], contract1, preferred_element_type=f32
            ) + lax.dot_general(
                upre[r0 : r0 + m, :], wu_ref[cols(k), :], contract1, preferred_element_type=f32
            )
            back[0:m, cols(k, width)] = dx.astype(bf16)
            return total + jnp.sum(
                y * cot_rows[0:m, cols(k)].astype(f32), axis=1, keepdims=True
            )

        dots = over_chunks(produce, jnp.zeros((m, 1), f32))
        for i, (j, _) in enumerate(entries):
            mark, sel = marks[i]
            lane = jnp.sum(
                jnp.where(sel, dots[i * cap : (i + 1) * cap], 0.0), axis=0, keepdims=True
            )
            gates[j] = mark * lane

    def spread(d):
        for i, (j, _) in enumerate(batch_slots(d)):
            def put(k, carry, i=i, j=j):
                for base in (0, width):
                    slots[j, :, cols(k, base)] = lax.dot_general(
                        sel_buf[j], back[i * cap : (i + 1) * cap, cols(k, base)], contract0,
                        preferred_element_type=f32,
                    ).astype(bf16)
                return carry

            over_chunks(put)

    started = {}

    def begin(key, copies):
        started[key] = copies
        for c in copies:
            c.start()

    def got(key):
        for c in started[key]:
            c.wait_recv()

    def sent(key):
        for c in started[key]:
            c.wait_send()

    def finish(d):
        if d < half:
            sent(("ag", d + 1))
        for o in offsets(d):
            sent(("twin", o))
        spread(d)
        for o in offsets(d):
            begin(("part", o), partial_copies(o))

    begin(("ag", 1), gather_copies(1))
    begin(("twin", 0), twin_copies(0))
    for c in loads[3:]:
        c.wait()
    got(("twin", 0))
    compute(0)
    for s in range(1, half + 1):
        got(("ag", s))
        if s < half:
            begin(("ag", s + 1), gather_copies(s + 1))
        for o in offsets(s):
            begin(("twin", o), twin_copies(o))
        finish(s - 1)
        for o in offsets(s):
            got(("twin", o))
        compute(s)
    finish(half)

    def add_into(o, arrived, bases):
        def body(k, carry):
            for base, extra in zip((0, width), bases):
                total = slots[o, :, cols(k, base)].astype(f32) + sib[o, :, cols(k, base)].astype(f32)
                for side, step in extra:
                    total = total + ring[side, step, :, cols(k, base)].astype(f32)
                slots[o, :, cols(k, base)] = total.astype(bf16)
            return carry

        over_chunks(body)
        tile = gates[o] + sib_t[o]
        for side, step in arrived:
            tile = tile + ring_t[side, step]
        gates[o] = tile

    def weight_grads(which):
        out, rhs = ((og_ref, gpre), (ou_ref, upre), (od_ref, None))[which]

        def body(k, carry):
            c = pl.ds(pl.multiple_of(k * 256, 256), 256)
            if rhs is not None:
                out[c, :] = lax.dot_general(
                    rows[:, c], rhs[...], contract0, preferred_element_type=f32
                ).astype(bf16)
            else:
                c2 = pl.ds(pl.multiple_of(width + k * 256, 256), 256)
                out[:, c] = lax.dot_general(
                    hid[...], rows[:, c2], contract0, preferred_element_type=f32
                ).astype(bf16)
            return carry

        lax.fori_loop(0, width // 256, body, 0)

    for s in range(1, half + 1):
        o = half + 1 - s
        i = s - 1
        if s == 1:
            got(("part", o))
            add_into(o, [], ([], []))
            begin(("rs", s), [
                remote(slots.at[o, :, lo], ring.at[0, i, :, lo], rs_send.at[0, i], rs_recv.at[0, i], right),
                remote(slots.at[o, :, hi], ring.at[1, i, :, hi], rs_send.at[1, i], rs_recv.at[1, i], left),
                remote(gates.at[o], ring_t.at[0, i], rst_send.at[0, i], rst_recv.at[0, i], right),
            ])
        else:
            n = (-o) % chips
            got(("part", o))
            got(("part", n))
            got(("rs", s - 1))
            here = [[(0, i - 1)], [(1, i - 1)]]
            add_into(o, here[0], (here[0], here[0] if s > 2 else []))
            copies = [
                remote(slots.at[o], ring.at[0, i], rs_send.at[0, i], rs_recv.at[0, i], right),
                remote(gates.at[o], ring_t.at[0, i], rst_send.at[0, i], rst_recv.at[0, i], right),
                remote(slots.at[n], ring.at[1, i], rs_send.at[1, i], rs_recv.at[1, i], left),
                remote(gates.at[n], ring_t.at[1, i], rst_send.at[1, i], rst_recv.at[1, i], left),
            ]
            for c in copies[:2]:
                c.start()
            add_into(n, here[1] if s > 2 else [], (here[1] if s > 2 else [], here[1]))
            for c in copies[2:]:
                c.start()
            started[("rs", s)] = copies
        if s <= 3:
            weight_grads(s - 1)
    got(("part", 0))
    got(("rs", half))
    last = half - 1

    def final(k, carry):
        for out, base in ((eo_ref, 0), (gt_ref, width)):
            out[:, cols(k)] = (
                slots[0, :, cols(k, base)].astype(f32)
                + sib[0, :, cols(k, base)].astype(f32)
                + ring[0, last, :, cols(k, base)].astype(f32)
                + ring[1, last, :, cols(k, base)].astype(f32)
            ).astype(bf16)
        return carry

    over_chunks(final)
    gg_ref[...] = gates[0] + sib_t[0] + ring_t[0, last] + ring_t[1, last]
    for o in range(chips):
        sent(("part", o))
    for s in range(1, half + 1):
        sent(("rs", s))


def ring_layer(y_size, tokens, cotangent, route_ids, gate_probs, w_gate, w_up, w_down):
    owners = lax.axis_size("owner")
    chips = owners // 2
    half = chips // 2
    tok, width = tokens.shape
    routes = route_ids.shape[1]
    ffw = w_gate.shape[2]
    cap = -(-(2 * tok * routes // owners) // 16) * 16
    cap = min(cap, tok)
    bf16, f32 = jnp.bfloat16, jnp.float32
    route_t = jnp.pad(
        route_ids.reshape(owners, tok, routes).transpose(0, 2, 1),
        ((0, 0), (0, 8 - routes), (0, 0)), constant_values=-1,
    )
    prob_t = jnp.pad(gate_probs.T, ((0, 8 - routes), (0, 0)))
    vmem = pl.BlockSpec(memory_space=pltpu.VMEM)
    hbm = pl.BlockSpec(memory_space=pl.ANY)
    dma = pltpu.SemaphoreType.DMA
    total = owners * cap
    ring_sems = [dma((2, half))] * 4
    chip_sems = [dma((chips,))] * 4
    eo, gt, gg, og, ou, od = pl.pallas_call(
        functools.partial(ring_kernel, y_size, owners, cap),
        out_shape=(
            jax.ShapeDtypeStruct((tok, width), bf16),
            jax.ShapeDtypeStruct((tok, width), bf16),
            jax.ShapeDtypeStruct((8, tok), f32),
            jax.ShapeDtypeStruct((width, ffw), bf16),
            jax.ShapeDtypeStruct((width, ffw), bf16),
            jax.ShapeDtypeStruct((ffw, width), bf16),
        ),
        in_specs=[vmem, hbm, hbm, hbm, hbm, hbm, hbm],
        out_specs=(vmem,) * 6,
        scratch_shapes=[
            pltpu.VMEM((owners, tok, 2 * width), bf16),
            pltpu.VMEM((owners, 8, tok), f32),
            pltpu.VMEM((chips, tok, 2 * width), bf16),
            pltpu.VMEM((chips, 8, tok), f32),
            pltpu.VMEM((2, half, tok, 2 * width), bf16),
            pltpu.VMEM((2, half, 8, tok), f32),
            pltpu.VMEM((owners, 8, tok), f32),
            pltpu.VMEM((owners, cap, tok), bf16),
            pltpu.VMEM((total, 2 * width), bf16),
            pltpu.VMEM((4 * cap, width), bf16),
            pltpu.VMEM((4 * cap, 1), f32),
            pltpu.VMEM((4 * cap, 2 * width), bf16),
            pltpu.VMEM((total, ffw), bf16),
            pltpu.VMEM((total, ffw), bf16),
            pltpu.VMEM((total, ffw), bf16),
            pltpu.VMEM((width, ffw), bf16),
            pltpu.VMEM((width, ffw), bf16),
            pltpu.VMEM((ffw, width), bf16),
        ] + ring_sems + chip_sems + chip_sems + ring_sems + [dma((6,))],
        compiler_params=pltpu.CompilerParams(
            collective_id=0, has_side_effects=True, vmem_limit_bytes=62 * 2**20
        ),
        cost_estimate=pl.CostEstimate(
            flops=18 * total * width * ffw, bytes_accessed=16 * width * ffw, transcendentals=0
        ),
        name="ring_layer",
    )(route_t, prob_t, tokens, cotangent, w_gate[0], w_up[0], w_down[0])
    return eo, gt, gg[:routes].T, og[None], ou[None], od[None]


def solution(mesh):
    owners = mesh.shape["owner"]
    chips = owners // 2
    y_size = ring_width(mesh)

    def run(tokens, cotangent, route_ids, gate_probs, w_gate, w_up, w_down):
        block = tokens.shape[0] * tokens.shape[1] * 4
        fits = owners * 2 * block <= 36 * 2**20
        if not fits or owners % 2 or chips < 4 or chips % 2:
            return local(tokens, cotangent, route_ids, gate_probs, w_gate, w_up, w_down)
        return ring_layer(
            y_size, tokens, cotangent, route_ids, gate_probs, w_gate, w_up, w_down
        )

    placed = (
        P(("group", "owner"), None),
        P(("group", "owner"), None),
        P("group", None),
        P(("group", "owner"), None),
        P("owner", None, None),
        P("owner", None, None),
        P("owner", None, None),
    )
    return jax.shard_map(
        run,
        mesh=mesh,
        in_specs=placed,
        out_specs=(
            P(("group", "owner"), None),
            P(("group", "owner"), None),
            P(("group", "owner"), None),
            P(("group", "owner"), None, None),
            P(("group", "owner"), None, None),
            P(("group", "owner"), None, None),
        ),
        check_vma=False,
    )
```

```python
import functools

import jax
import jax.numpy as jnp
from jax import lax
from jax.experimental import pallas as pl
from jax.experimental.pallas import tpu as pltpu
from jax.sharding import PartitionSpec as P


def expert_pass(tokens_in, cotan_in, gate_w, up_w, down_w):
    gate_pre = jnp.dot(tokens_in, gate_w, preferred_element_type=jnp.float32)
    up_pre = jnp.dot(tokens_in, up_w, preferred_element_type=jnp.float32)
    gate_sig = jax.nn.sigmoid(gate_pre)
    gate_act = gate_pre * gate_sig
    hidden = (gate_act * up_pre).astype(jnp.bfloat16)
    expert_y = jnp.dot(hidden, down_w, preferred_element_type=jnp.float32).astype(jnp.bfloat16)
    d_hidden = jnp.dot(cotan_in, down_w.T, preferred_element_type=jnp.float32)
    grad_gate_pre = (d_hidden * up_pre * gate_sig * (1.0 + gate_pre * (1.0 - gate_sig))).astype(
        jnp.bfloat16
    )
    grad_up_pre = (d_hidden * gate_act).astype(jnp.bfloat16)
    expert_dx = (
        jnp.dot(grad_gate_pre, gate_w.T, preferred_element_type=jnp.float32)
        + jnp.dot(grad_up_pre, up_w.T, preferred_element_type=jnp.float32)
    ).astype(jnp.bfloat16)
    return (expert_y, expert_dx, hidden, grad_gate_pre, grad_up_pre)


def running_sum(flags):
    count = flags.shape[0]
    at = jnp.arange(count, dtype=jnp.int32)
    lower = (at[:, None] >= at[None, :]).astype(jnp.bfloat16)
    return jnp.dot(
        lower, flags.astype(jnp.bfloat16), preferred_element_type=jnp.float32
    ).astype(jnp.int32)


def local(tokens, cotangent, route_ids, gate_probs, w_gate, w_up, w_down):
    owner_count = lax.axis_size("owner")
    my_index = lax.axis_index("owner")
    token_rows, model_width = tokens.shape
    route_count = route_ids.shape[1]
    slot_depth = 2 * token_rows * route_count // owner_count
    assign_count = token_rows * route_count
    slot_total = owner_count * slot_depth
    expert_ids = jnp.arange(owner_count, dtype=jnp.int32)
    id_table = route_ids.reshape(owner_count, assign_count)
    my_routes = lax.dynamic_index_in_dim(id_table, my_index, 0, keepdims=False)
    one_hot = (my_routes[:, None] == expert_ids[None, :]).astype(jnp.int32)
    rank_within = jnp.sum((running_sum(one_hot) - one_hot) * one_hot, axis=1)
    source_loads = jnp.sum((id_table == my_index).astype(jnp.int32), axis=1)
    scaled_cot = (gate_probs[:, :, None] * cotangent[:, None, :].astype(jnp.float32)).astype(
        jnp.bfloat16
    )
    token_copies = jnp.broadcast_to(tokens[:, None, :], (token_rows, route_count, model_width))
    zero_row = jnp.zeros((1, model_width), jnp.bfloat16)
    token_ext = jnp.concatenate([token_copies.reshape(assign_count, model_width), zero_row], axis=0)
    cotan_ext = jnp.concatenate([scaled_cot.reshape(assign_count, model_width), zero_row], axis=0)
    is_hot = jnp.zeros((assign_count,), dtype=bool)
    slot_target = jnp.where(is_hot, slot_total, my_routes * slot_depth + rank_within)
    slot_source = jnp.full((slot_total + 1,), assign_count, jnp.int32)
    slot_source = slot_source.at[slot_target].set(jnp.arange(assign_count, dtype=jnp.int32))[
        :slot_total
    ]
    send_tokens = token_ext[slot_source].reshape(owner_count, slot_depth, model_width)
    send_cotan = cotan_ext[slot_source].reshape(owner_count, slot_depth, model_width)
    got_tokens, got_cotan = (
        lax.all_to_all(send_tokens, "owner", split_axis=0, concat_axis=0, tiled=True),
        lax.all_to_all(send_cotan, "owner", split_axis=0, concat_axis=0, tiled=True),
    )
    live_slot = (jnp.arange(slot_depth, dtype=jnp.int32)[None, :] < source_loads[:, None]).reshape(
        slot_total
    )
    compact_pos = running_sum(live_slot.astype(jnp.int32)[:, None])[:, 0] - 1
    live_total = jnp.sum(source_loads)
    compact_from = jnp.full((slot_total,), slot_total, jnp.int32)
    compact_from = compact_from.at[jnp.where(live_slot, compact_pos, slot_total)].set(
        jnp.arange(slot_total, dtype=jnp.int32), mode="drop"
    )
    flat_tokens = jnp.concatenate([got_tokens.reshape(slot_total, model_width), zero_row], axis=0)
    flat_cotan = jnp.concatenate([got_cotan.reshape(slot_total, model_width), zero_row], axis=0)
    compact_tokens = flat_tokens[compact_from]
    compact_cotan = flat_cotan[compact_from]
    gate_w = w_gate[0]
    up_w = w_up[0]
    down_w = w_down[0]
    hidden_width = gate_w.shape[1]

    def block_step(turn_index, carried):
        out_rows, back_rows, grad_gate, grad_up, grad_down = carried
        row_start = turn_index * assign_count
        block_tokens = lax.dynamic_slice_in_dim(compact_tokens, row_start, assign_count, 0)
        block_cotan = lax.dynamic_slice_in_dim(compact_cotan, row_start, assign_count, 0)
        expert_y, expert_dx, hidden, grad_gate_pre, grad_up_pre = expert_pass(
            block_tokens, block_cotan, gate_w, up_w, down_w
        )
        out_rows = lax.dynamic_update_slice_in_dim(out_rows, expert_y, row_start, 0)
        back_rows = lax.dynamic_update_slice_in_dim(back_rows, expert_dx, row_start, 0)
        grad_gate = grad_gate + jnp.dot(
            block_tokens.T, grad_gate_pre, preferred_element_type=jnp.float32
        )
        grad_up = grad_up + jnp.dot(block_tokens.T, grad_up_pre, preferred_element_type=jnp.float32)
        grad_down = grad_down + jnp.dot(hidden.T, block_cotan, preferred_element_type=jnp.float32)
        return (out_rows, back_rows, grad_gate, grad_up, grad_down)

    turn_count = (live_total + assign_count - 1) // assign_count
    initial = (
        jnp.zeros((slot_total, model_width), jnp.bfloat16),
        jnp.zeros((slot_total, model_width), jnp.bfloat16),
        jnp.zeros((model_width, hidden_width), jnp.float32),
        jnp.zeros((model_width, hidden_width), jnp.float32),
        jnp.zeros((hidden_width, model_width), jnp.float32),
    )
    out_rows, back_rows, grad_gate, grad_up, grad_down = lax.fori_loop(
        0, turn_count, block_step, initial
    )
    return_pos = jnp.where(live_slot, compact_pos, 0)
    return_y = out_rows[return_pos].reshape(owner_count, slot_depth, model_width)
    return_dx = back_rows[return_pos].reshape(owner_count, slot_depth, model_width)
    came_y, came_dx = (
        lax.all_to_all(return_y, "owner", split_axis=0, concat_axis=0, tiled=True),
        lax.all_to_all(return_dx, "owner", split_axis=0, concat_axis=0, tiled=True),
    )
    pick_slot = jnp.where(is_hot, 0, slot_target)
    routed_rows = came_y.reshape(slot_total, model_width)[pick_slot]
    routed_backs = came_dx.reshape(slot_total, model_width)[pick_slot]
    grad_gate_out = grad_gate.astype(jnp.bfloat16)
    grad_up_out = grad_up.astype(jnp.bfloat16)
    grad_down_out = grad_down.astype(jnp.bfloat16)
    routed_y = routed_rows.reshape(token_rows, route_count, model_width).astype(jnp.float32)
    expert_out = jnp.sum(gate_probs[:, :, None] * routed_y, axis=1).astype(jnp.bfloat16)
    grad_tokens = jnp.sum(
        routed_backs.reshape(token_rows, route_count, model_width).astype(jnp.float32), axis=1
    ).astype(jnp.bfloat16)
    grad_gates = jnp.sum(routed_y * cotangent[:, None, :].astype(jnp.float32), axis=2)
    return (
        expert_out,
        grad_tokens,
        grad_gates,
        grad_gate_out[None],
        grad_up_out[None],
        grad_down_out[None],
    )


def ring_width(mesh):
    coords = [getattr(d, "coords", None) for d in mesh.devices.reshape(mesh.devices.shape[0], -1)[0]]
    if any(c is None for c in coords):
        return 2
    return 2 if len({c[1] for c in coords}) == 2 else 1


def ring_kernel(
    y_size, owners, cap,
    route_ref, prob_ref, tok_ref, cot_ref, wg_hbm, wu_hbm, wd_hbm,
    eo_ref, gt_ref, gg_ref, og_ref, ou_ref, od_ref,
    slots, probs, sib, sib_t, ring, ring_t, gates, sel_buf, rows, cot_rows, prow, back,
    hid, gpre, upre, wg_ref, wu_ref, wd_ref,
    ag_send, ag_recv, agt_send, agt_recv, sf_send, sf_recv, sft_send, sft_recv,
    sp_send, sp_recv, spt_send, spt_recv, rs_send, rs_recv, rst_send, rst_recv, loc,
):
    f32, bf16 = jnp.float32, jnp.bfloat16
    chips = owners // 2
    half = chips // 2
    depth = chips // y_size
    tok, width = tok_ref.shape
    me = lax.axis_index("owner")
    chip = me // 2
    core = me % 2
    if y_size == 2:
        cz, cy = chip // 2, chip % 2
        pos = (1 - cy) * cz + cy * (2 * depth - 1 - cz)
    else:
        pos = chip

    def owner_at(offset, core_index):
        p = (pos + offset + chips) % chips
        if y_size == 2:
            py = p // depth
            pz = (1 - py) * p + py * (2 * depth - 1 - p)
            return (pz * 2 + py) * 2 + core_index
        return p * 2 + core_index

    right, left, twin = owner_at(1, core), owner_at(-1, core), owner_at(0, 1 - core)

    loads = [
        pltpu.make_async_copy(tok_ref, slots.at[0, :, pl.ds(0, width)], loc.at[0]),
        pltpu.make_async_copy(cot_ref, slots.at[0, :, pl.ds(width, width)], loc.at[1]),
        pltpu.make_async_copy(prob_ref, probs.at[0], loc.at[2]),
        pltpu.make_async_copy(wg_hbm, wg_ref, loc.at[3]),
        pltpu.make_async_copy(wu_hbm, wu_ref, loc.at[4]),
        pltpu.make_async_copy(wd_hbm, wd_ref, loc.at[5]),
    ]
    for c in loads:
        c.start()
    barrier = pltpu.get_barrier_semaphore()
    for other in (right, left, twin):
        pl.semaphore_signal(
            barrier, inc=1, device_id={"owner": other}, device_id_type=pl.DeviceIdType.MESH
        )
    pl.semaphore_wait(barrier, 3)
    for c in loads[:3]:
        c.wait()

    def remote(src, dst, send, recv, to):
        return pltpu.make_async_remote_copy(
            src_ref=src, dst_ref=dst, send_sem=send, recv_sem=recv,
            device_id={"owner": to}, device_id_type=pl.DeviceIdType.MESH,
        )

    lo, hi = pl.ds(0, width), pl.ds(width, width)

    def gather_copies(s, part):
        a, b = (-(s - 1)) % chips, s - 1
        c, d = (-s) % chips, s
        i = s - 1
        span = (lo, hi)[part]
        out = []
        if s < half or part == 0:
            out.append(remote(
                slots.at[a, :, span], slots.at[c, :, span],
                ag_send.at[0, i, part], ag_recv.at[0, i, part], right,
            ))
        if s < half or part == 1:
            out.append(remote(
                slots.at[b, :, span], slots.at[d, :, span],
                ag_send.at[1, i, part], ag_recv.at[1, i, part], left,
            ))
        if part == 0:
            out.append(remote(probs.at[a], probs.at[c], agt_send.at[0, i], agt_recv.at[0, i], right))
            if s < half:
                out.append(remote(probs.at[b], probs.at[d], agt_send.at[1, i], agt_recv.at[1, i], left))
        return out

    def twin_copies(o):
        return [
            remote(slots.at[o], slots.at[chips + o], sf_send.at[o], sf_recv.at[o], twin),
            remote(probs.at[o], probs.at[chips + o], sft_send.at[o], sft_recv.at[o], twin),
        ]

    def partial_copies(o):
        return [
            remote(slots.at[chips + o], sib.at[o], sp_send.at[o], sp_recv.at[o], twin),
            remote(gates.at[chips + o], sib_t.at[o], spt_send.at[o], spt_recv.at[o], twin),
        ]

    def offsets(d):
        return [d] if d in (0, half) else [(-d) % chips, d]

    first_row = [0] * (half + 1)
    for d in range(half):
        first_row[d + 1] = first_row[d] + 2 * cap * len(offsets(d))
    chunk = 512 if width % 512 == 0 else 128
    contract0 = (((0,), (0,)), ((), ()))
    contract1 = (((1,), (1,)), ((), ()))

    def cols(i, base=0):
        return pl.ds(pl.multiple_of(base + i * chunk, 128), chunk)

    def over_chunks(body, init=0):
        return lax.fori_loop(0, width // chunk, body, init)

    upper = (
        lax.broadcasted_iota(jnp.int32, (tok, tok), 0)
        <= lax.broadcasted_iota(jnp.int32, (tok, tok), 1)
    ).astype(bf16)

    def batch_slots(d):
        return [(o, core) for o in offsets(d)] + [(chips + o, 1 - core) for o in offsets(d)]

    def compute(d):
        r0 = first_row[d]
        entries = batch_slots(d)
        m = cap * len(entries)
        marks = []
        for i, (j, source_core) in enumerate(entries):
            owner = owner_at(j % chips, source_core)
            mark = (route_ref[owner] == me).astype(f32)
            hit = jnp.sum(mark, axis=0, keepdims=True)
            count = jnp.dot(
                jnp.broadcast_to(hit, (8, tok)).astype(bf16), upper, preferred_element_type=f32
            )[0:1]
            rank = jnp.where(hit > 0, count - 1, -1.0)
            sel = lax.broadcasted_iota(jnp.int32, (cap, tok), 0).astype(f32) == rank
            weight = jnp.sum(probs[j] * mark, axis=0, keepdims=True)
            prow[i * cap : (i + 1) * cap, :] = jnp.sum(
                jnp.where(sel, weight, 0.0), axis=1, keepdims=True
            )
            sel_buf[j] = sel.astype(bf16)
            marks.append((mark, sel))

            def pick(k, carry, i=i, j=j):
                s = sel_buf[j]
                rows[r0 + i * cap : r0 + (i + 1) * cap, cols(k)] = jnp.dot(
                    s, slots[j, :, cols(k)], preferred_element_type=f32
                ).astype(bf16)
                c = jnp.dot(s, slots[j, :, cols(k, width)], preferred_element_type=f32)
                cot_rows[i * cap : (i + 1) * cap, cols(k)] = c.astype(bf16)
                rows[r0 + i * cap : r0 + (i + 1) * cap, cols(k, width)] = (
                    c * prow[i * cap : (i + 1) * cap, :]
                ).astype(bf16)
                return carry

            over_chunks(pick)
        x = rows[r0 : r0 + m, 0:width]
        gate_pre = jnp.dot(x, wg_ref[...], preferred_element_type=f32)
        up_pre = jnp.dot(x, wu_ref[...], preferred_element_type=f32)
        sig = jax.nn.sigmoid(gate_pre)
        act = gate_pre * sig
        hid[r0 : r0 + m, :] = (act * up_pre).astype(bf16)
        d_hidden = lax.dot_general(
            rows[r0 : r0 + m, width : 2 * width], wd_ref[...], contract1,
            preferred_element_type=f32,
        )
        gpre[r0 : r0 + m, :] = (
            d_hidden * up_pre * sig * (1.0 + gate_pre * (1.0 - sig))
        ).astype(bf16)
        upre[r0 : r0 + m, :] = (d_hidden * act).astype(bf16)

        def produce(k, total):
            y = jnp.dot(
                hid[r0 : r0 + m, :], wd_ref[:, cols(k)], preferred_element_type=f32
            ).astype(bf16).astype(f32)
            back[0:m, cols(k)] = (y * prow[0:m, :]).astype(bf16)
            dx = lax.dot_general(
                gpre[r0 : r0 + m, :], wg_ref[cols(k), :], contract1, preferred_element_type=f32
            ) + lax.dot_general(
                upre[r0 : r0 + m, :], wu_ref[cols(k), :], contract1, preferred_element_type=f32
            )
            back[0:m, cols(k, width)] = dx.astype(bf16)
            return total + jnp.sum(
                y * cot_rows[0:m, cols(k)].astype(f32), axis=1, keepdims=True
            )

        dots = over_chunks(produce, jnp.zeros((m, 1), f32))
        for i, (j, _) in enumerate(entries):
            mark, sel = marks[i]
            lane = jnp.sum(
                jnp.where(sel, dots[i * cap : (i + 1) * cap], 0.0), axis=0, keepdims=True
            )
            gates[j] = mark * lane

    def spread(d):
        for i, (j, _) in enumerate(batch_slots(d)):
            def put(k, carry, i=i, j=j):
                for base in (0, width):
                    slots[j, :, cols(k, base)] = lax.dot_general(
                        sel_buf[j], back[i * cap : (i + 1) * cap, cols(k, base)], contract0,
                        preferred_element_type=f32,
                    ).astype(bf16)
                return carry

            over_chunks(put)

    started = {}

    def begin(key, copies):
        started[key] = copies
        for c in copies:
            c.start()

    def got(key):
        for c in started[key]:
            c.wait_recv()

    def sent(key):
        for c in started[key]:
            c.wait_send()

    def finish(d):
        if d < half:
            sent(("ag", d + 1, 0))
            sent(("ag", d + 1, 1))
        for o in offsets(d):
            sent(("twin", o))
        spread(d)
        for o in offsets(d):
            begin(("part", o), partial_copies(o))

    for part in (0, 1):
        begin(("ag", 1, part), gather_copies(1, part))
    begin(("twin", 0), twin_copies(0))
    for c in loads[3:]:
        c.wait()
    got(("twin", 0))
    compute(0)
    for s in range(1, half + 1):
        for part in (0, 1):
            got(("ag", s, part))
            if s < half:
                begin(("ag", s + 1, part), gather_copies(s + 1, part))
        for o in offsets(s):
            begin(("twin", o), twin_copies(o))
        finish(s - 1)
        for o in offsets(s):
            got(("twin", o))
        compute(s)
    finish(half)

    def add_into(o, base, arrived):
        def body(k, carry):
            total = slots[o, :, cols(k, base)].astype(f32) + sib[o, :, cols(k, base)].astype(f32)
            for side, step in arrived:
                total = total + ring[side, step, :, cols(k, base)].astype(f32)
            slots[o, :, cols(k, base)] = total.astype(bf16)
            return carry

        over_chunks(body)

    def add_tile(o, arrived):
        tile = gates[o] + sib_t[o]
        for side, step in arrived:
            tile = tile + ring_t[side, step]
        gates[o] = tile

    def send_sum(side, s, part):
        o = half + 1 - s if side == 0 else (s - half - 1) % chips
        i = s - 1
        to = right if side == 0 else left
        arrived = []
        if ("rs", side, s - 1, part) in started:
            got(("rs", side, s - 1, part))
            arrived = [(side, s - 2)]
        add_into(o, part * width, arrived)
        span = (lo, hi)[part]
        copies = [remote(
            slots.at[o, :, span], ring.at[side, i, :, span],
            rs_send.at[side, i, part], rs_recv.at[side, i, part], to,
        )]
        if (side == 0 or s > 1) and part == side:
            add_tile(o, arrived if side == 0 or s > 2 else [])
            copies.append(remote(
                gates.at[o], ring_t.at[side, i], rst_send.at[side, i], rst_recv.at[side, i], to,
            ))
        begin(("rs", side, s, part), copies)

    def weight_grads(which):
        out, rhs = ((og_ref, gpre), (ou_ref, upre), (od_ref, None))[which]

        def body(k, carry):
            c = pl.ds(pl.multiple_of(k * 256, 256), 256)
            if rhs is not None:
                out[c, :] = lax.dot_general(
                    rows[:, c], rhs[...], contract0, preferred_element_type=f32
                ).astype(bf16)
            else:
                c2 = pl.ds(pl.multiple_of(width + k * 256, 256), 256)
                out[:, c] = lax.dot_general(
                    hid[...], rows[:, c2], contract0, preferred_element_type=f32
                ).astype(bf16)
            return carry

        lax.fori_loop(0, width // 256, body, 0)

    got(("part", half))
    send_sum(0, 1, 0)
    send_sum(1, 1, 1)
    for s in range(2, half + 1):
        for o in offsets(half + 1 - s):
            got(("part", o))
        send_sum(0, s, 1)
        send_sum(1, s, 0)
        if s <= 4:
            weight_grads(s - 2)
        send_sum(0, s, 0)
        send_sum(1, s, 1)
    for which in range(max(half - 1, 0), 3):
        weight_grads(which)
    got(("part", 0))
    for side, part in ((0, 1), (1, 0), (0, 0), (1, 1)):
        got(("rs", side, half, part))
    last = half - 1

    def final(k, carry):
        for out, base in ((eo_ref, 0), (gt_ref, width)):
            out[:, cols(k)] = (
                slots[0, :, cols(k, base)].astype(f32)
                + sib[0, :, cols(k, base)].astype(f32)
                + ring[0, last, :, cols(k, base)].astype(f32)
                + ring[1, last, :, cols(k, base)].astype(f32)
            ).astype(bf16)
        return carry

    over_chunks(final)
    gg_ref[...] = gates[0] + sib_t[0] + ring_t[0, last] + ring_t[1, last]
    for o in range(chips):
        sent(("part", o))
    for key in list(started):
        if key[0] == "rs":
            sent(key)


def ring_layer(y_size, tokens, cotangent, route_ids, gate_probs, w_gate, w_up, w_down):
    owners = lax.axis_size("owner")
    chips = owners // 2
    half = chips // 2
    tok, width = tokens.shape
    routes = route_ids.shape[1]
    ffw = w_gate.shape[2]
    cap = -(-(2 * tok * routes // owners) // 16) * 16
    cap = min(cap, tok)
    bf16, f32 = jnp.bfloat16, jnp.float32
    route_t = jnp.pad(
        route_ids.reshape(owners, tok, routes).transpose(0, 2, 1),
        ((0, 0), (0, 8 - routes), (0, 0)), constant_values=-1,
    )
    prob_t = jnp.pad(gate_probs.T, ((0, 8 - routes), (0, 0)))
    vmem = pl.BlockSpec(memory_space=pltpu.VMEM)
    hbm = pl.BlockSpec(memory_space=pl.ANY)
    dma = pltpu.SemaphoreType.DMA
    total = owners * cap
    part_sems = [dma((2, half, 2))] * 2
    ring_sems = part_sems + [dma((2, half))] * 2
    chip_sems = [dma((chips,))] * 4
    eo, gt, gg, og, ou, od = pl.pallas_call(
        functools.partial(ring_kernel, y_size, owners, cap),
        out_shape=(
            jax.ShapeDtypeStruct((tok, width), bf16),
            jax.ShapeDtypeStruct((tok, width), bf16),
            jax.ShapeDtypeStruct((8, tok), f32),
            jax.ShapeDtypeStruct((width, ffw), bf16),
            jax.ShapeDtypeStruct((width, ffw), bf16),
            jax.ShapeDtypeStruct((ffw, width), bf16),
        ),
        in_specs=[vmem, hbm, hbm, hbm, hbm, hbm, hbm],
        out_specs=(vmem,) * 6,
        scratch_shapes=[
            pltpu.VMEM((owners, tok, 2 * width), bf16),
            pltpu.VMEM((owners, 8, tok), f32),
            pltpu.VMEM((chips, tok, 2 * width), bf16),
            pltpu.VMEM((chips, 8, tok), f32),
            pltpu.VMEM((2, half, tok, 2 * width), bf16),
            pltpu.VMEM((2, half, 8, tok), f32),
            pltpu.VMEM((owners, 8, tok), f32),
            pltpu.VMEM((owners, cap, tok), bf16),
            pltpu.VMEM((total, 2 * width), bf16),
            pltpu.VMEM((4 * cap, width), bf16),
            pltpu.VMEM((4 * cap, 1), f32),
            pltpu.VMEM((4 * cap, 2 * width), bf16),
            pltpu.VMEM((total, ffw), bf16),
            pltpu.VMEM((total, ffw), bf16),
            pltpu.VMEM((total, ffw), bf16),
            pltpu.VMEM((width, ffw), bf16),
            pltpu.VMEM((width, ffw), bf16),
            pltpu.VMEM((ffw, width), bf16),
        ] + ring_sems + chip_sems + chip_sems + ring_sems + [dma((6,))],
        compiler_params=pltpu.CompilerParams(
            collective_id=0, has_side_effects=True, vmem_limit_bytes=62 * 2**20
        ),
        cost_estimate=pl.CostEstimate(
            flops=18 * total * width * ffw, bytes_accessed=16 * width * ffw, transcendentals=0
        ),
        name="ring_layer",
    )(route_t, prob_t, tokens, cotangent, w_gate[0], w_up[0], w_down[0])
    return eo, gt, gg[:routes].T, og[None], ou[None], od[None]


def solution(mesh):
    owners = mesh.shape["owner"]
    chips = owners // 2
    y_size = ring_width(mesh)

    def run(tokens, cotangent, route_ids, gate_probs, w_gate, w_up, w_down):
        block = tokens.shape[0] * tokens.shape[1] * 4
        fits = owners * 2 * block <= 36 * 2**20
        if not fits or owners % 2 or chips < 4 or chips % 2:
            return local(tokens, cotangent, route_ids, gate_probs, w_gate, w_up, w_down)
        return ring_layer(
            y_size, tokens, cotangent, route_ids, gate_probs, w_gate, w_up, w_down
        )

    placed = (
        P(("group", "owner"), None),
        P(("group", "owner"), None),
        P("group", None),
        P(("group", "owner"), None),
        P("owner", None, None),
        P("owner", None, None),
        P("owner", None, None),
    )
    return jax.shard_map(
        run,
        mesh=mesh,
        in_specs=placed,
        out_specs=(
            P(("group", "owner"), None),
            P(("group", "owner"), None),
            P(("group", "owner"), None),
            P(("group", "owner"), None, None),
            P(("group", "owner"), None, None),
            P(("group", "owner"), None, None),
        ),
        check_vma=False,
    )
```
